32 devices in a mesh: judge: 2 (over y), gx: 4 (over z), gy: 2 (over core), gz: 2 (over x).
Axes of the slice: x: 2, y: 2, z: 4, core: 2. Of those that a mesh axis runs over, the one named last changes fastest.
Arguments:
- tokens: bfloat16 [2048, 8192], P(('judge', 'gy'), ('gz', 'gx')), parts along dimension 0, may hold values from -6 to 6
- out_grad: bfloat16 [2048, 8192], P(('judge', 'gy'), ('gz', 'gx')), parts along dimension 0, may hold values from -6 to 6
- gate_weight: bfloat16 [8192, 14336], P(('gz', 'gy'), 'gx'), may hold values from -0.09375 to 0.09375
- up_weight: bfloat16 [8192, 14336], P(('gz', 'gy'), 'gx'), may hold values from -0.0625 to 0.0625
- down_weight: bfloat16 [14336, 8192], P('gx', ('gz', 'gy')), may hold values from -0.046875 to 0.046875
Outputs:
- input_grad: bfloat16 [2048, 8192], P(('judge', 'gy'), ('gz', 'gx')), parts along dimension 0
- gate_grad: bfloat16 [16384, 14336], P(('judge', 'gz', 'gy'), 'gx'), parts along dimension 0
- up_grad: bfloat16 [16384, 14336], P(('judge', 'gz', 'gy'), 'gx'), parts along dimension 0
The draws below stay inside these ranges and needn't reach their ends.
There are 2 independent parts, one for each index of `judge`. The reference program is written for one: setup_inputs(seed, part) draws one part's arguments, and reference() takes and returns one part's arrays. A program takes and returns all parts, laid end to end along the dimension named above; an argument that names none is the same for every part. Nothing has to cross between parts.
All inputs are finite; a program needn't handle non-finite values.
Results may differ from the reference program's by a relative error of at most 0.0051.
Values may be sent and summed in bfloat16 or wider, within the bound.
A program may use at most 384 MiB of HBM per device.

```python
import jax
import jax.numpy as jnp
from jax import lax

D = 8192
FF = 14336
TOKENS = 1024


def spiked(entries, rng, source, target, shards_of, factor):
    owner, partner = [(jnp.arange(entries.shape[position]) // (entries.shape[position] // shards_of)).reshape([-1 if axis == position else 1 for axis in range(entries.ndim)]) for position in (source, target)]
    chosen = jax.random.permutation(rng, shards_of)[partner]
    strong = (owner == chosen) | (owner == (partner + shards_of // 2) % shards_of)
    return jnp.where(strong, factor * entries, entries)


def levels(key, shape, cuts, low, top_value):
    def one(dim, blocks):
        draws = jax.random.uniform(jax.random.fold_in(jax.random.fold_in(key, 6), dim), (blocks,), jnp.float32, low / len(cuts), top_value / len(cuts))
        return jnp.repeat(jnp.exp(draws), shape[dim] // blocks).reshape((-1,) + (1,) * (len(shape) - dim - 1))

    level = one(*cuts[0])
    for cut in cuts[1:]:
        level = level * one(*cut)
    return level


def normal_values(key, dims, scale, reach, shards=(), dtype=jnp.bfloat16):
    level = levels(key, dims, shards, -0.22, 0.18) if shards else 1.0
    entries = jax.random.normal(key, dims, jnp.float32) * scale * level
    return jnp.minimum(jnp.maximum(entries, -reach), reach).astype(dtype)


def heavy_noise(stream_key, dims, deviation, limit, split, heavy, dtype=jnp.bfloat16):
    drawn = deviation * jax.random.normal(stream_key, dims, jnp.float32)
    if split:
        drawn = drawn * levels(stream_key, dims, split, -0.22, 0.18)
    return jnp.clip(spiked(drawn, jax.random.fold_in(stream_key, 3), *heavy), -limit, limit).astype(dtype)


def setup_inputs(seed: int = 0, part: int = 0) -> dict:
    streams_of = jax.random.split(jax.random.key(seed), 6)
    part_splits = jax.random.split(jax.random.fold_in(streams_of[5], part), 6)
    tokens = normal_values(part_splits[0], (TOKENS, D), 1.0, 6.0, ((0, 2), (1, 8)))
    out_grad = normal_values(part_splits[1], (TOKENS, D), 1.0, 6.0, ((0, 2), (1, 8)))
    gate_weight = heavy_noise(streams_of[2], (D, FF), D ** -0.5, 0.09375, ((0, 4), (1, 4)), (1, 0, 4, 2.0))
    up_weight = normal_values(streams_of[3], (D, FF), D ** -0.5, 0.0625, ((0, 4), (1, 4)))
    down_weight = normal_values(streams_of[4], (FF, D), FF ** -0.5, 0.046875, ((0, 4), (1, 4)))
    return dict(tokens=tokens, out_grad=out_grad, gate_weight=gate_weight, up_weight=up_weight, down_weight=down_weight)


def swiglu_back(gate_sum, up_sum, back_sum):
    sigmoid_gate = jax.nn.sigmoid(gate_sum)
    grad_up = (back_sum * gate_sum * sigmoid_gate).astype(jnp.bfloat16)
    grad_gate = (back_sum * up_sum * sigmoid_gate * (1.0 + gate_sum * (1.0 - sigmoid_gate))).astype(jnp.bfloat16)
    return grad_gate, grad_up


def contract_last(left, right):
    return lax.dot_general(left, right, (((1,), (1,)), ((), ())), preferred_element_type=jnp.float32)


def contract_first(left, right):
    return lax.dot_general(left, right, (((0,), (0,)), ((), ())), preferred_element_type=jnp.float32)


def reference(tokens, out_grad, gate_weight, up_weight, down_weight):
    gate_sum = jnp.dot(tokens, gate_weight, preferred_element_type=jnp.float32)
    up_sum = jnp.dot(tokens, up_weight, preferred_element_type=jnp.float32)
    back_sum = contract_last(out_grad, down_weight)
    grad_gate, grad_up = swiglu_back(gate_sum, up_sum, back_sum)
    input_grad = (contract_last(grad_gate, gate_weight) + contract_last(grad_up, up_weight)).astype(jnp.bfloat16)
    weight_scale = float(TOKENS) ** -0.5
    gate_grad = (contract_first(tokens, grad_gate) * weight_scale).astype(jnp.bfloat16)
    up_grad = (contract_first(tokens, grad_up) * weight_scale).astype(jnp.bfloat16)
    return input_grad, gate_grad, up_grad
```

```python
import jax
import jax.numpy as jnp
from jax import lax
from jax.sharding import PartitionSpec as P

CHUNKS = 4


def swiglu_back(gate_sum, up_sum, back_sum):
    sigmoid_gate = jax.nn.sigmoid(gate_sum)
    grad_up = (back_sum * gate_sum * sigmoid_gate).astype(jnp.bfloat16)
    grad_gate = (back_sum * up_sum * sigmoid_gate * (1.0 + gate_sum * (1.0 - sigmoid_gate))).astype(
        jnp.bfloat16
    )
    return (grad_gate, grad_up)


def contract_last(left, right):
    return lax.dot_general(
        left, right, (((1,), (1,)), ((), ())), preferred_element_type=jnp.float32
    )


def contract_first(left, right):
    return lax.dot_general(
        left, right, (((0,), (0,)), ((), ())), preferred_element_type=jnp.float32
    )


def shift(block, axis, step):
    count = lax.axis_size(axis)
    return lax.ppermute(block, axis, [(i, (i + step) % count) for i in range(count)])


def block_of(array, index, size, dim=0):
    return lax.dynamic_slice_in_dim(array, index * size, size, dim)


def scatter_sum(total, axis):
    count, me = lax.axis_size(axis), lax.axis_index(axis)
    size = total.shape[0] // count
    own = block_of(total, me, size)
    for step in range(1, count):
        away = block_of(total, lax.rem(me + step, count), size).astype(jnp.bfloat16)
        own = own + shift(away, axis, step).astype(jnp.float32)
    return own


def gather_rows(block, axis):
    count, me = lax.axis_size(axis), lax.axis_index(axis)
    size = block.shape[0]
    if count == 2:
        other = shift(block, axis, 1)
        first = me == 0
        return jnp.concatenate(
            [jnp.where(first, block, other), jnp.where(first, other, block)], axis=0
        )
    whole = jnp.zeros((count * size,) + block.shape[1:], block.dtype)
    whole = lax.dynamic_update_slice_in_dim(whole, block, me * size, 0)
    for step in range(1, count):
        got = shift(block, axis, step)
        source = lax.rem(me + count - step, count)
        whole = lax.dynamic_update_slice_in_dim(whole, got, source * size, 0)
    return whole


def per_device(tokens, out_grad, gate_weight, up_weight, down_weight):
    rows, shard = tokens.shape
    weight_scale = float(rows * lax.axis_size("gy")) ** (-0.5)
    width = gate_weight.shape[0]
    shards = width // shard
    gy = lax.axis_index("gy")
    chunk = rows // CHUNKS

    def load(index):
        pair = jnp.stack(
            [
                tokens[index * chunk : (index + 1) * chunk],
                out_grad[index * chunk : (index + 1) * chunk],
            ]
        )
        blocks = lax.all_gather(pair, "gx", axis=0)
        mine = block_of(blocks, gy, shards)
        other = shift(block_of(blocks, 1 - gy, shards), "gy", 1)
        both = jnp.concatenate([mine, other], axis=2)
        both = both.transpose(1, 2, 0, 3).reshape(2, 2 * chunk, width)
        return both[0], both[1]

    def core_sum(part):
        return part[:chunk] + shift(part[chunk:], "gy", 1)

    def sums(features, grads):
        out = []
        for left, weight, dot in (
            (features, gate_weight, lambda a, b: jnp.dot(a, b, preferred_element_type=jnp.float32)),
            (features, up_weight, lambda a, b: jnp.dot(a, b, preferred_element_type=jnp.float32)),
            (grads, down_weight, contract_last),
        ):
            out.append(scatter_sum(core_sum(dot(left, weight)), "gz"))
        return out

    def spread(grad):
        half = gather_rows(grad, "gz")
        return jnp.concatenate([half, shift(half, "gy", 1)], axis=0)

    def input_rows(grad_gate, grad_up):
        part = contract_last(grad_gate, gate_weight) + contract_last(grad_up, up_weight)
        part = part.astype(jnp.bfloat16)
        mine, other = part[:chunk], shift(part[chunk:], "gy", 1)
        first = gy == 0
        whole = jnp.concatenate(
            [jnp.where(first, mine, other), jnp.where(first, other, mine)], axis=1
        )
        count, me = lax.axis_size("gx"), lax.axis_index("gx")
        if count > 8:
            total = lax.psum_scatter(
                whole.astype(jnp.float32), "gx", scatter_dimension=1, tiled=True
            )
            return total.astype(jnp.bfloat16)
        total = block_of(whole, me, shard, 1).astype(jnp.float32)
        for step in range(1, count):
            away = block_of(whole, lax.rem(me + step, count), shard, 1)
            total = total + shift(away, "gx", step).astype(jnp.float32)
        return total.astype(jnp.bfloat16)

    features, gates, ups, inputs = [], [], [], []
    for index in range(CHUNKS):
        feature, grad = load(index)
        grad_gate, grad_up = swiglu_back(*sums(feature, grad))
        grad_gate, grad_up = spread(grad_gate), spread(grad_up)
        inputs.append(input_rows(grad_gate, grad_up))
        features.append(feature)
        gates.append(grad_gate)
        ups.append(grad_up)
    features = jnp.concatenate(features, axis=0)
    gate_total = contract_first(features, jnp.concatenate(gates, axis=0))
    up_total = contract_first(features, jnp.concatenate(ups, axis=0))
    gate_grad = (gate_total * weight_scale).astype(jnp.bfloat16)
    up_grad = (up_total * weight_scale).astype(jnp.bfloat16)
    return (jnp.concatenate(inputs, axis=0), gate_grad, up_grad)


def solution(mesh):
    return jax.shard_map(
        per_device,
        mesh=mesh,
        in_specs=(
            P(("judge", "gy"), ("gz", "gx")),
            P(("judge", "gy"), ("gz", "gx")),
            P(("gz", "gy"), "gx"),
            P(("gz", "gy"), "gx"),
            P("gx", ("gz", "gy")),
        ),
        out_specs=(
            P(("judge", "gy"), ("gz", "gx")),
            P(("judge", "gz", "gy"), "gx"),
            P(("judge", "gz", "gy"), "gx"),
        ),
        check_vma=False,
    )
```

```python
import jax
import jax.numpy as jnp
from jax import lax
from jax.sharding import PartitionSpec as P

CHUNKS = 4


def swiglu_back(gate_sum, up_sum, back_sum):
    sigmoid_gate = jax.nn.sigmoid(gate_sum)
    grad_up = (back_sum * gate_sum * sigmoid_gate).astype(jnp.bfloat16)
    grad_gate = (back_sum * up_sum * sigmoid_gate * (1.0 + gate_sum * (1.0 - sigmoid_gate))).astype(
        jnp.bfloat16
    )
    return (grad_gate, grad_up)


def contract_last(left, right):
    return lax.dot_general(
        left, right, (((1,), (1,)), ((), ())), preferred_element_type=jnp.float32
    )


def contract_first(left, right):
    return lax.dot_general(
        left, right, (((0,), (0,)), ((), ())), preferred_element_type=jnp.float32
    )


def shift(block, axis, step):
    count = lax.axis_size(axis)
    return lax.ppermute(block, axis, [(i, (i + step) % count) for i in range(count)])


def block_of(array, index, size, dim=0):
    return lax.dynamic_slice_in_dim(array, index * size, size, dim)


def after(values, earlier):
    if not earlier:
        return values
    return lax.optimization_barrier((values, earlier))[0]


def scatter_parts(totals, axis):
    count, me = lax.axis_size(axis), lax.axis_index(axis)
    size = totals[0].shape[0] // count
    received = []
    for step in range(1, count):
        block = lax.rem(me + step, count)
        away = [block_of(total, block, size).astype(jnp.bfloat16) for total in totals]
        received.append(shift(jnp.stack(away), axis, step))
    return [block_of(total, me, size) for total in totals], received


def add_blocks(blocks):
    total = blocks[0].astype(jnp.float32)
    for block in blocks[1:]:
        total = total + block.astype(jnp.float32)
    return total.astype(jnp.bfloat16)


def send_rows(block, axis):
    return [shift(block, axis, step) for step in range(1, lax.axis_size(axis))]


def gather_rows(block, received, axis):
    count, me = lax.axis_size(axis), lax.axis_index(axis)
    size = block.shape[1]
    if count == 2:
        other = received[0]
        first = me == 0
        return jnp.concatenate(
            [jnp.where(first, block, other), jnp.where(first, other, block)], axis=1
        )
    whole = jnp.zeros((block.shape[0], count * size) + block.shape[2:], block.dtype)
    whole = lax.dynamic_update_slice_in_dim(whole, block, me * size, 1)
    for step, got in enumerate(received, 1):
        source = lax.rem(me + count - step, count)
        whole = lax.dynamic_update_slice_in_dim(whole, got, source * size, 1)
    return whole


def per_device(tokens, out_grad, gate_weight, up_weight, down_weight):
    rows, shard = tokens.shape
    weight_scale = float(rows * lax.axis_size("gy")) ** (-0.5)
    width = gate_weight.shape[0]
    shards = width // shard
    gy = lax.axis_index("gy")
    chunk = rows // CHUNKS

    def fetch(index):
        pair = jnp.stack(
            [
                tokens[index * chunk : (index + 1) * chunk],
                out_grad[index * chunk : (index + 1) * chunk],
            ]
        )
        return lax.all_gather(pair, "gx", axis=0)

    def load(blocks):
        mine = block_of(blocks, gy, shards)
        other = shift(block_of(blocks, 1 - gy, shards), "gy", 1)
        both = jnp.concatenate([mine, other], axis=2)
        both = both.transpose(1, 2, 0, 3).reshape(2, 2 * chunk, width)
        return both[0], both[1]

    def dots(features, grads, pending):
        parts = [
            jnp.dot(features, gate_weight, preferred_element_type=jnp.float32),
            jnp.dot(features, up_weight, preferred_element_type=jnp.float32),
        ]
        if pending is not None:
            spreads.append(spread(*after(pending, parts)))
            grads = after(grads, [spreads[-1][0]])
        parts.append(contract_last(grads, down_weight))
        away = shift(jnp.stack([part[chunk:] for part in parts]), "gy", 1)
        return [part[:chunk] for part in parts], away

    def send_sums(owns, others):
        return scatter_parts([own + others[i] for i, own in enumerate(owns)], "gz")

    def spread(pair, received):
        half = gather_rows(pair, received, "gz")
        return half, shift(half, "gy", 1)

    def input_part(grad_gate, grad_up):
        part = contract_last(grad_gate, gate_weight) + contract_last(grad_up, up_weight)
        part = part.astype(jnp.bfloat16)
        return part[:chunk], shift(part[chunk:], "gy", 1)

    def send_inputs(mine, other):
        first = gy == 0
        whole = jnp.concatenate(
            [jnp.where(first, mine, other), jnp.where(first, other, mine)], axis=1
        )
        count, me = lax.axis_size("gx"), lax.axis_index("gx")
        if count > 8:
            return [
                lax.psum_scatter(whole.astype(jnp.float32), "gx", scatter_dimension=1, tiled=True)
            ]
        blocks = [block_of(whole, me, shard, 1)]
        for step in range(1, count):
            away = block_of(whole, lax.rem(me + step, count), shard, 1)
            blocks.append(shift(away, "gx", step))
        return blocks

    blocks = [fetch(0)]
    loaded = [load(blocks[0])]
    summed, spreads, grads, in_parts, in_blocks, inputs = [], [], [], [], [], []
    last, pending = None, None
    for turn in range(CHUNKS + 2):
        if turn < CHUNKS:
            pairs = dots(*after(loaded[turn], last), pending)
            last = pairs[0]
            if turn + 1 < CHUNKS:
                blocks.append(fetch(turn + 1))
                loaded.append(load(after(blocks[turn + 1], last)))
        if turn >= 2:
            mine, other = after(spreads[turn - 2], last)
            grads.append([jnp.concatenate([mine[i], other[i]], axis=0) for i in range(2)])
            in_parts.append(input_part(*grads[-1]))
            last = [in_parts[-1][0]]
        if turn >= 3:
            in_blocks.append(send_inputs(*after(in_parts[turn - 3], last)))
        if turn >= 4:
            inputs.append(add_blocks(after(in_blocks[turn - 4], last)))
        if 1 <= turn <= CHUNKS:
            totals, received = after(summed[turn - 1], last)
            for got in received:
                totals = [total + got[i].astype(jnp.float32) for i, total in enumerate(totals)]
            small = swiglu_back(*totals)
            pending = (jnp.stack(small), send_rows(jnp.stack(small), "gz"))
            if turn + 1 >= CHUNKS:
                spreads.append(spread(*pending))
            last = list(small)
        if turn < CHUNKS:
            summed.append(send_sums(*after(pairs, last)))
            last = summed[-1][0]
    features = jnp.concatenate([pair[0] for pair in loaded], axis=0)
    gates = jnp.concatenate([pair[0] for pair in grads], axis=0)
    ups = jnp.concatenate([pair[1] for pair in grads], axis=0)
    gate_total = contract_first(features, after(gates, last))
    gate_grad = (gate_total * weight_scale).astype(jnp.bfloat16)
    in_blocks.append(send_inputs(*in_parts[-1]))
    inputs.append(add_blocks(after(in_blocks[-2], [gate_grad])))
    up_total = contract_first(features, after(ups, [gate_grad]))
    up_grad = (up_total * weight_scale).astype(jnp.bfloat16)
    inputs.append(add_blocks(after(in_blocks[-1], [up_grad])))
    return (jnp.concatenate(inputs, axis=0), gate_grad, up_grad)


def solution(mesh):
    return jax.shard_map(
        per_device,
        mesh=mesh,
        in_specs=(
            P(("judge", "gy"), ("gz", "gx")),
            P(("judge", "gy"), ("gz", "gx")),
            P(("gz", "gy"), "gx"),
            P(("gz", "gy"), "gx"),
            P("gx", ("gz", "gy")),
        ),
        out_specs=(
            P(("judge", "gy"), ("gz", "gx")),
            P(("judge", "gz", "gy"), "gx"),
            P(("judge", "gz", "gy"), "gx"),
        ),
        check_vma=False,
    )
```
